256 devices in a mesh: wide: 64 (over x, y_lo, z), narrow: 4 (over y_hi, core).
Axes of the slice: x: 4, y: 4 (y_hi: 2, y_lo: 2; y = y_hi * 2 + y_lo), z: 8, core: 2. Of those that a mesh axis runs over, the one named last changes fastest.
Arguments:
- tokens: bfloat16 [16384, 3584], P(('wide', 'narrow')), may hold values from -6 to 6
- positions: int32 [16384], P(('wide', 'narrow')), may hold values from 0 to 16383, as said below
- gain: float32 [3584], replicated, may hold values from 0.5 to 1.5
- w_qkv: bfloat16 [3584, 2304], P('narrow'), as said below
- projection_bias: float32 [2304], replicated, may hold values from -3 to 3
Outputs:
- context: bfloat16 [16384, 1792], P(('wide', 'narrow'))
The draws below stay inside these ranges and needn't reach their ends.
Inputs may be any that keep to these rules, and one draw needn't show every extreme that they name: Every aligned block of 32 tokens holds 32 consecutive positions in rising order, and each position of 0 to 16383 occurs once. `w_qkv`: entries of mean zero.
All inputs are finite; a program needn't handle non-finite values.
Results may differ from the reference program's by a relative error of at most 0.012.
The reference program's roundings to bfloat16 on the way count: a program that leaves them out, or rounds other values in their place, can miss the bound.
Values may be sent and summed in bfloat16 or wider, within the bound.
No kernel may reach another device: no remote copies, remote signals or barrier semaphores. Data moves between devices by JAX's collectives and lax.ppermute only.
A program may use at most 192 MiB of HBM per device.

```python
import jax
import jax.numpy as jnp
from jax import lax

MODEL_WIDTH = 3584
QUERY_HEADS = 14
KEY_VALUE_HEADS = 2
HEAD_SIZE = 128
HALF = 32
SEQ = 16384


def draw_positions(key, part):
    key = jax.random.fold_in(key, 11)
    order = jax.random.permutation(key, SEQ // HALF)
    index = jnp.arange(SEQ, dtype=jnp.int32)
    return (order[index // HALF] * HALF + index % HALF).astype(jnp.int32)


def draw_w_qkv(key, part):
    key = jax.random.fold_in(key, 12)
    rotary_base = jax.random.normal(key, (MODEL_WIDTH, (QUERY_HEADS + 2 * KEY_VALUE_HEADS) * HEAD_SIZE), jnp.float32) * MODEL_WIDTH ** (-0.5)
    return rotary_base.astype(jnp.bfloat16)


def shard_levels(key, shape, pieces, smallest, top_value):
    loudness = 1.0
    for axis_at, parts in pieces:
        steps = jax.random.uniform(jax.random.fold_in(jax.random.fold_in(key, 6), axis_at), (parts,), jnp.float32, smallest / len(pieces), top_value / len(pieces))
        loudness = loudness * jnp.repeat(jnp.exp(steps), shape[axis_at] // parts).reshape((-1,) + (1,) * (len(shape) - 1 - axis_at))
    return loudness


def bell_draw(rng, dims, width, bound, split=(), held_as=jnp.bfloat16):
    drawn = width * jax.random.normal(rng, dims, jnp.float32)
    if split:
        drawn = drawn * shard_levels(rng, dims, split, -0.22, 0.18)
    return jnp.clip(drawn, -bound, bound).astype(held_as)


def setup_inputs(seed: int = 0) -> dict:
    key_list = jax.random.split(jax.random.key(seed), 6)
    tokens = bell_draw(key_list[0], (SEQ, MODEL_WIDTH), 1.0, 6.0, ((0, 256),))
    positions = draw_positions(jax.random.fold_in(key_list[5], 71), 0)
    gain = jnp.clip(1.0 + 0.1 * jax.random.normal(key_list[2], (MODEL_WIDTH,), jnp.float32), 0.5, 1.5)
    w_qkv = draw_w_qkv(jax.random.fold_in(key_list[5], 71), 0)
    projection_bias = bell_draw(key_list[4], ((QUERY_HEADS + 2 * KEY_VALUE_HEADS) * HEAD_SIZE,), 0.5, 3.0, (), jnp.float32)
    return {"tokens": tokens, "positions": positions, "gain": gain, "w_qkv": w_qkv, "projection_bias": projection_bias}


def apply_rotary(x, pos):
    half = x.shape[-1] // 2
    steps = jnp.arange(half, dtype=jnp.float32) * (2.0 / x.shape[-1])
    inverse = jnp.power(jnp.float32(10000000.0), -steps)
    angles = pos.astype(jnp.float32)[:, None] * inverse[None, :]
    cosine = jnp.concatenate([jnp.cos(angles), jnp.cos(angles)], axis=1)[:, None, :]
    sine = jnp.concatenate([jnp.sin(angles), jnp.sin(angles)], axis=1)[:, None, :]
    turned = jnp.concatenate([-x[..., half:], x[..., :half]], axis=-1)
    return x * cosine + turned * sine

def project(tokens, positions, gain, w_qkv, projection_bias):
    values = tokens.astype(jnp.float32)
    spread = lax.optimization_barrier(jnp.mean(values * values, axis=1, keepdims=True))
    normed = (values * lax.rsqrt(spread + 1e-06) * gain[None, :]).astype(jnp.bfloat16)
    projected_rows = jnp.dot(normed, w_qkv, preferred_element_type=jnp.float32) + projection_bias[None, :]
    row_count = tokens.shape[0]
    query = apply_rotary(projected_rows[:, :QUERY_HEADS * HEAD_SIZE].reshape(row_count, QUERY_HEADS, HEAD_SIZE), positions).astype(jnp.bfloat16)
    key_rows = apply_rotary(projected_rows[:, QUERY_HEADS * HEAD_SIZE:(QUERY_HEADS + KEY_VALUE_HEADS) * HEAD_SIZE].reshape(row_count, KEY_VALUE_HEADS, HEAD_SIZE), positions).astype(jnp.bfloat16)
    value_rows = projected_rows[:, (QUERY_HEADS + KEY_VALUE_HEADS) * HEAD_SIZE:].reshape(row_count, KEY_VALUE_HEADS, HEAD_SIZE).astype(jnp.bfloat16)
    return (query, key_rows, value_rows)

def reference(tokens, positions, gain, w_qkv, projection_bias):
    query, key_rows, value_rows = project(tokens, positions, gain, w_qkv, projection_bias)
    query_block = min(256, SEQ)
    scale = 1.0 / HEAD_SIZE ** 0.5
    head_group = QUERY_HEADS // KEY_VALUE_HEADS
    key_f = key_rows.astype(jnp.float32)
    val_f = value_rows.astype(jnp.float32)

    def one_block(item):
        query_tile, p_blk = item
        query_float = query_tile.astype(jnp.float32).reshape(query_block, KEY_VALUE_HEADS, head_group, HEAD_SIZE)
        scores = jnp.einsum('qcgd,kcd->qcgk', query_float, key_f) * scale
        allowed = positions[None, None, None, :] <= p_blk[:, None, None, None]
        top = lax.optimization_barrier(jnp.max(jnp.where(allowed, scores, -jnp.inf), axis=-1))
        weights = jnp.where(allowed, jnp.exp(scores - top[..., None]), 0.0)
        total = lax.optimization_barrier(jnp.sum(weights, axis=-1))
        probs = weights.astype(jnp.bfloat16).astype(jnp.float32)
        summed = jnp.einsum('qcgk,kcd->qcgd', probs, val_f)
        return (summed / total[..., None]).astype(jnp.bfloat16).reshape(query_block, QUERY_HEADS * HEAD_SIZE)
    q_blocks = query.reshape(SEQ // query_block, query_block, QUERY_HEADS, HEAD_SIZE)
    p_blocks = positions.reshape(SEQ // query_block, query_block)
    out = lax.map(one_block, (q_blocks, p_blocks))
    return out.reshape(SEQ, QUERY_HEADS * HEAD_SIZE)
```

```python
import functools

import jax
import jax.numpy as jnp
from jax import lax
from jax.experimental import pallas as pl
from jax.experimental.pallas import tpu as pltpu
from jax.sharding import Mesh
from jax.sharding import PartitionSpec as P

AXES = ("x", "yl", "z", "yh", "core")
SIZES = (4, 2, 8, 2, 2)
WIDTH = 3584
HALF_WIDTH = WIDTH // 2
QUARTER = WIDTH // 4
HEADS = 14
GROUP = 7
HEAD = 128
QCOLS = HEADS * HEAD
CCOLS = GROUP * HEAD
ROWS = 64
PAIR_ROWS = 2 * ROWS
NEG = -1e30
SCALE_LOG2 = (1.0 / HEAD**0.5) * 1.4426950408889634

F32 = jnp.float32
BF16 = jnp.bfloat16
VM = pl.BlockSpec(memory_space=pltpu.VMEM)
SM = pl.BlockSpec(memory_space=pltpu.SMEM)


def shape(dims, dtype):
    return jax.ShapeDtypeStruct(dims, dtype)


def call(kernel, out_shape, args, specs, scratch=(), flops=0, nbytes=0, aliases=None):
    many = isinstance(out_shape, (list, tuple))
    return pl.pallas_call(
        kernel,
        out_shape=out_shape,
        in_specs=specs,
        out_specs=[VM] * len(out_shape) if many else VM,
        scratch_shapes=list(scratch),
        input_output_aliases=aliases or {},
        compiler_params=pltpu.CompilerParams(vmem_limit_bytes=48 * 2**20),
        cost_estimate=pl.CostEstimate(flops=flops, bytes_accessed=nbytes, transcendentals=0),
    )(*args)


def norm_kernel(ids, tokens, gain, keep, send):
    values = tokens[...].astype(F32)
    spread = jnp.mean(values * values, axis=1, keepdims=True)
    normed = (values * lax.rsqrt(spread + 1e-06) * gain[...]).astype(BF16)
    low, high = normed[:, :HALF_WIDTH], normed[:, HALF_WIDTH:]

    @pl.when(ids[0] == 0)
    def _():
        keep[...] = low
        send[...] = high

    @pl.when(ids[0] == 1)
    def _():
        keep[...] = high
        send[...] = low


def key_part_kernel(ids, keep, came, w_own, w_other, x_own, x_other, part_keep, part_send, rows):
    yh, core = ids[0], ids[1]
    rows[pl.ds(pl.multiple_of(yh * ROWS, ROWS), ROWS), :] = keep[...]
    rows[pl.ds(pl.multiple_of((1 - yh) * ROWS, ROWS), ROWS), :] = came[...]
    x_own[...] = rows[:, pl.ds(pl.multiple_of(core * QUARTER, 128), QUARTER)]
    x_other[...] = rows[:, pl.ds(pl.multiple_of((1 - core) * QUARTER, 128), QUARTER)]
    part = jnp.dot(x_own[...], w_own[:, QCOLS:], preferred_element_type=F32)
    part += jnp.dot(x_other[...], w_other[:, QCOLS:], preferred_element_type=F32)

    def put(first, second):
        for ref, c in ((first, 0), (second, 1)):
            ref[:, :HEAD] = part[:, c * HEAD : (c + 1) * HEAD]
            ref[:, HEAD:] = part[:, (2 + c) * HEAD : (3 + c) * HEAD]

    @pl.when(yh == 0)
    def _():
        put(part_keep, part_send)

    @pl.when(yh == 1)
    def _():
        put(part_send, part_keep)


def query_part_kernel(ids, x_own, x_other, w_own, w_other, part_keep, part_send):
    yh = ids[0]
    for c in range(2):
        cols = slice(c * CCOLS, (c + 1) * CCOLS)
        part = jnp.dot(x_own[...], w_own[:, cols], preferred_element_type=F32)
        part += jnp.dot(x_other[...], w_other[:, cols], preferred_element_type=F32)

        @pl.when(yh == c)
        def _():
            part_keep[...] = part

        @pl.when(yh != c)
        def _():
            part_send[...] = part


def rotate(x, cosine, sine):
    return x * cosine + pltpu.roll(x, HEAD // 2, 1) * sine


def key_finish_kernel(ids, part_keep, part_came, bias, cosine, sine, pos_a, pos_b, out_a, out_b):
    yh = ids[0]
    k_bias = bias[:, pl.ds(pl.multiple_of(QCOLS + yh * HEAD, HEAD), HEAD)]
    v_bias = bias[:, pl.ds(pl.multiple_of(QCOLS + (2 + yh) * HEAD, HEAD), HEAD)]
    total = part_keep[...] + part_came[...]
    keys = rotate(total[:, :HEAD] + k_bias, cosine[...], sine[...]).astype(BF16)
    values = (total[:, HEAD:] + v_bias).astype(BF16)
    for ref, pos, start in ((out_a, pos_a, 0), (out_b, pos_b, ROWS)):
        for i in range(ref.shape[0]):
            ref[i, :ROWS, :HEAD] = keys[start : start + ROWS]
            ref[i, :ROWS, HEAD:] = values[start : start + ROWS]
            ref[i, ROWS:, :] = pos[...]


def query_finish_kernel(ids, part_keep, part_came, bias, cosine, sine, out):
    yh = ids[0]
    for h in range(GROUP):
        cols = slice(h * HEAD, (h + 1) * HEAD)
        here = bias[:, pl.ds(pl.multiple_of(yh * CCOLS + h * HEAD, HEAD), HEAD)]
        x = part_keep[:, cols] + part_came[:, cols] + here
        out[h] = rotate(x, cosine[...], sine[...]).astype(BF16)


def pack_kernel(gathered, out):
    count = gathered.shape[0]
    row = lax.broadcasted_iota(jnp.int32, (16, 2 * HEAD), 0)
    marks = jnp.zeros((16, 2 * HEAD), F32)
    for i in range(count):
        out[i * ROWS : (i + 1) * ROWS, :] = gathered[i, :ROWS, :]
        here = gathered[i, ROWS:, :].astype(F32)
        marks += jnp.where(row == i // 2, jnp.broadcast_to(here[:1, :], marks.shape), 0.0)
    out[count * ROWS :, :] = marks.astype(BF16)


def attend_kernel(first, last, n_pieces, *refs):
    refs = list(refs)
    q_own, q_other, q_pos = refs[:3]
    refs = refs[3:]
    if not first:
        m_in, acc_in = refs[:2]
        refs = refs[2:]
    pieces, refs = refs[:n_pieces], refs[n_pieces:]
    if last:
        own, other, m_ref, acc_ref = refs
    else:
        m_ref, acc_ref = refs
    if first:
        m_ref[...] = jnp.full(m_ref.shape, NEG, F32)
        acc_ref[...] = jnp.zeros(acc_ref.shape, F32)
    elif last:
        m_ref[...] = m_in[...]
        acc_ref[...] = acc_in[...]
    positions = q_pos[...]
    for piece in pieces:
        count = piece.shape[0] - 16
        keys = piece[:count, :HEAD]
        values = jnp.concatenate([piece[:count, HEAD:], jnp.ones((count, HEAD), BF16)], axis=1)
        marks = piece[count:, :].astype(F32)
        marks = marks[:, :HEAD] * 128.0 + marks[:, HEAD:]
        k_pos = jnp.concatenate([marks[i : i + 1, :] for i in range(count // HEAD)], axis=1)
        fill = jnp.where(positions >= k_pos, 0.0, NEG)
        for h in range(GROUP):
            for part, q in ((0, q_own), (1, q_other)):
                rows = slice(part * PAIR_ROWS, (part + 1) * PAIR_ROWS)
                scores = lax.dot_general(
                    q[h], keys, (((1,), (1,)), ((), ())), preferred_element_type=F32
                )
                scores = scores * SCALE_LOG2 + fill[rows]
                before = m_ref[h, rows, :]
                top = jnp.maximum(before, jnp.max(scores, axis=1, keepdims=True))
                m_ref[h, rows, :] = top
                weights = jnp.exp2(scores - top[:, :1]).astype(BF16)
                decay = jnp.exp2(before - top)
                decay = jnp.concatenate([decay, decay], axis=1)
                acc_ref[h, rows, :] = acc_ref[h, rows, :] * decay + jnp.dot(
                    weights, values, preferred_element_type=F32
                )
    if last:
        lane = lax.broadcasted_iota(jnp.int32, (PAIR_ROWS, HEAD), 1)
        for h in range(GROUP):
            for part, ref in ((0, own), (1, other)):
                rows = slice(part * PAIR_ROWS, (part + 1) * PAIR_ROWS)
                ref[h, :, :HEAD] = acc_ref[h, rows, :HEAD]
                ref[h, :, HEAD:] = jnp.where(
                    lane < HEAD // 2, acc_ref[h, rows, HEAD:], m_ref[h, rows, :]
                )


def attend(q_own, q_other, q_pos, state, pieces, last):
    first = state is None
    args = [q_own, q_other, q_pos] + ([] if first else list(state)) + list(pieces)
    keys = sum(p.shape[0] - 16 for p in pieces)
    m_shape = (GROUP, 2 * PAIR_ROWS, HEAD)
    acc_shape = (GROUP, 2 * PAIR_ROWS, 2 * HEAD)
    scratch = ()
    if last:
        outs = [shape((GROUP, PAIR_ROWS, 2 * HEAD), F32)] * 2
        scratch = (pltpu.VMEM(m_shape, F32), pltpu.VMEM(acc_shape, F32))
        aliases = None
    else:
        outs = [shape(m_shape, F32), shape(acc_shape, F32)]
        aliases = None if first else {3: 0, 4: 1}
    return call(
        functools.partial(attend_kernel, first, last, len(pieces)),
        outs,
        args,
        [VM] * len(args),
        scratch,
        flops=GROUP * 2 * PAIR_ROWS * keys * HEAD * 10,
        nbytes=keys * 512,
        aliases=aliases,
    )


def combine_kernel(ids, own, came, keep, send):
    yh = ids[0]
    for h in range(GROUP):
        num_a, num_b = own[h, :, :HEAD], came[h, :, :HEAD]
        l_a, l_b = own[h, :, HEAD : HEAD + 1], came[h, :, HEAD : HEAD + 1]
        m_a, m_b = own[h, :, 2 * HEAD - 1 :], came[h, :, 2 * HEAD - 1 :]
        top = jnp.maximum(m_a, m_b)
        s_a, s_b = jnp.exp2(m_a - top), jnp.exp2(m_b - top)
        total = l_a * s_a + l_b * s_b
        out = ((num_a * s_a + num_b * s_b) / total).astype(BF16)
        cols = slice(h * HEAD, (h + 1) * HEAD)

        @pl.when(yh == 0)
        def _():
            keep[:, cols] = out[:ROWS]
            send[:, cols] = out[ROWS:]

        @pl.when(yh == 1)
        def _():
            keep[:, cols] = out[ROWS:]
            send[:, cols] = out[:ROWS]


def join_kernel(ids, keep, came, out):
    @pl.when(ids[0] == 0)
    def _():
        out[:, :CCOLS] = keep[...]
        out[:, CCOLS:] = came[...]

    @pl.when(ids[0] == 1)
    def _():
        out[:, :CCOLS] = came[...]
        out[:, CCOLS:] = keep[...]


def swap_pair(x):
    pairs = [(2 * a + b, 2 * (1 - a) + (1 - b)) for a in range(2) for b in range(2)]
    return lax.ppermute(x, ("yl", "yh"), pairs)


def swap_core(x):
    return lax.ppermute(x, "core", [(0, 1), (1, 0)])


def shift(x, axis, step):
    n = SIZES[AXES.index(axis)]
    return lax.ppermute(x, axis, [(i, (i + step) % n) for i in range(n)])


def position_rows(pos, side):
    high, low = (pos // 128).astype(BF16), (pos % 128).astype(BF16)
    none = jnp.zeros_like(high)
    row = jnp.where(
        side == 0,
        jnp.concatenate([high, none, low, none]),
        jnp.concatenate([none, high, none, low]),
    )
    return jnp.broadcast_to(row[None, :], (16, 2 * HEAD))


def local(tokens, positions, gain, w_qkv, projection_bias):
    yh = lax.axis_index("yh").astype(jnp.int32)
    core = lax.axis_index("core").astype(jnp.int32)
    ids = jnp.stack([yh, core])
    gain = gain[None, :]
    bias = projection_bias[None, :]

    w_other = swap_core(w_qkv)
    keep, send = call(
        norm_kernel,
        [shape((ROWS, HALF_WIDTH), BF16)] * 2,
        [ids, tokens, gain],
        [SM, VM, VM],
    )
    came = swap_pair(send)
    pos_came = swap_pair(positions)
    pos = jnp.where(
        yh == 0, jnp.concatenate([positions, pos_came]), jnp.concatenate([pos_came, positions])
    )
    pos_other = swap_core(pos)
    q_pos = jnp.concatenate([pos, pos_other]).astype(F32)[:, None]
    steps = jnp.arange(HEAD // 2, dtype=F32) * (2.0 / HEAD)
    inverse = jnp.power(F32(10000000.0), -steps)
    angles = pos.astype(F32)[:, None] * inverse[None, :]
    cosine = jnp.concatenate([jnp.cos(angles)] * 2, axis=1)
    sine = jnp.concatenate([-jnp.sin(angles), jnp.sin(angles)], axis=1)
    pos_a = position_rows(pos[:ROWS], lax.axis_index("yl"))
    pos_b = position_rows(pos[ROWS:], lax.axis_index("z") % 2)

    x_own, x_other, kv_keep, kv_send = call(
        key_part_kernel,
        [shape((PAIR_ROWS, QUARTER), BF16)] * 2 + [shape((PAIR_ROWS, 2 * HEAD), F32)] * 2,
        [ids, keep, came, w_qkv, w_other],
        [SM, VM, VM, VM, VM],
        [pltpu.VMEM((PAIR_ROWS, HALF_WIDTH), BF16)],
    )
    kv_came = swap_pair(kv_send)
    q_keep, q_send = call(
        query_part_kernel,
        [shape((PAIR_ROWS, CCOLS), F32)] * 2,
        [ids, x_own, x_other, w_qkv, w_other],
        [SM, VM, VM, VM, VM],
    )
    q_came = swap_pair(q_send)
    rep_a, rep_b = call(
        key_finish_kernel,
        [shape((8, ROWS + 16, 2 * HEAD), BF16), shape((16, ROWS + 16, 2 * HEAD), BF16)],
        [ids, kv_keep, kv_came, bias, cosine, sine, pos_a, pos_b],
        [SM] + [VM] * 7,
    )
    got_a = lax.all_to_all(rep_a, ("x", "yl"), 0, 0, tiled=True)
    a0 = call(pack_kernel, shape((8 * ROWS + 16, 2 * HEAD), BF16), [got_a], [VM])
    up, down = shift(a0, "z", 1), shift(a0, "z", -1)
    got_b = lax.all_to_all(rep_b, ("yl", "z"), 0, 0, tiled=True)
    b0 = call(pack_kernel, shape((16 * ROWS + 16, 2 * HEAD), BF16), [got_b], [VM])
    b_pieces = [shift(b0, "x", s) for s in (1, -1, 2)]
    a_pieces = [up, down]
    for _ in range(2):
        up, down = shift(up, "z", 1), shift(down, "z", -1)
        a_pieces += [up, down]
    a_pieces.append(shift(up, "z", 1))

    q_own = call(
        query_finish_kernel,
        shape((GROUP, PAIR_ROWS, HEAD), BF16),
        [ids, q_keep, q_came, bias, cosine, sine],
        [SM] + [VM] * 5,
    )
    q_other = swap_core(q_own)

    state = attend(q_own, q_other, q_pos, None, [a0, b0] + a_pieces[:2], False)
    state = attend(q_own, q_other, q_pos, state, a_pieces[2:6], False)
    own, other = attend(q_own, q_other, q_pos, state, [a_pieces[6]] + b_pieces, True)
    came = swap_core(other)
    out_keep, out_send = call(
        combine_kernel, [shape((ROWS, CCOLS), BF16)] * 2, [ids, own, came], [SM, VM, VM]
    )
    out_came = swap_pair(out_send)
    return call(
        join_kernel, shape((ROWS, QCOLS), BF16), [ids, out_keep, out_came], [SM, VM, VM]
    )


def solution(mesh):
    fine = Mesh(mesh.devices.reshape(SIZES), AXES)
    placed = (P(AXES, None), P(AXES), P(), P(("yh", "core"), None), P())
    return jax.shard_map(
        local, mesh=fine, in_specs=placed, out_specs=P(AXES, None), check_vma=False
    )
```
